256 devices in a mesh: row: 8 (over y, core), col: 32 (over x, z).
Axes of the slice: x: 4, y: 4, z: 8, core: 2. Of those that a mesh axis runs over, the one named last changes fastest.
Arguments:
- tokens: bfloat16 [512, 8192], P('col', 'row'), may hold values from -6 to 6
- out_grad: bfloat16 [512, 8192], P('col', 'row'), may hold values from -6 to 6
- gate_weight: bfloat16 [8192, 28672], P('row', 'col'), may hold values from -0.0625 to 0.0625
- up_weight: bfloat16 [8192, 28672], P('row', 'col'), may hold values from -0.0625 to 0.0625
- down_weight: bfloat16 [28672, 8192], P('col', 'row'), may hold values from -0.03125 to 0.03125
Outputs:
- input_grad: bfloat16 [512, 8192], P('col', 'row')
- gate_grad: bfloat16 [8192, 28672], P('row', 'col')
- up_grad: bfloat16 [8192, 28672], P('row', 'col')
- down_grad: bfloat16 [28672, 8192], P('col', 'row')
The draws below stay inside these ranges and needn't reach their ends.
All inputs are finite; a program needn't handle non-finite values.
Results may differ from the reference program's by a relative error of at most 0.005.
Values may be sent and summed in bfloat16 or wider, within the bound.
No kernel may reach another device: no remote copies, remote signals or barrier semaphores. Data moves between devices by JAX's collectives and lax.ppermute only.
A program may use at most 64 MiB of HBM per device.

```python
import jax
import jax.numpy as jnp
from jax import lax

D = 8192
FF = 28672
TOKENS = 512


def shard_levels(own_key, extent, pieces, low, high):
    gain, own = 1.0, jax.random.fold_in(own_key, 6)
    for dim, shards_of in pieces:
        heights = jnp.exp(jax.random.uniform(jax.random.fold_in(own, dim), (shards_of,), jnp.float32, low / len(pieces), high / len(pieces)))
        gain = gain * jnp.repeat(heights, extent[dim] // shards_of).reshape([-1 if axis == dim else 1 for axis in range(len(extent))])
    return gain


def centred(own_key, extent, spread, bound, shards=(), held_as=jnp.bfloat16):
    result = spread * jax.random.normal(own_key, extent, jnp.float32)
    if shards:
        result = result * shard_levels(own_key, extent, shards, -0.22, 0.18)
    return jnp.clip(result, -bound, bound).astype(held_as)


def setup_inputs(seed: int = 0) -> dict:
    seeds = jax.random.split(jax.random.key(seed), 6)
    tokens = centred(seeds[0], (TOKENS, D), 1.0, 6.0, ((0, 32), (1, 8)))
    out_grad = centred(seeds[1], (TOKENS, D), 1.0, 6.0, ((0, 32), (1, 8)))
    gate_weight = centred(seeds[2], (D, FF), D ** -0.5, 0.0625, ((0, 8), (1, 32)))
    up_weight = centred(seeds[3], (D, FF), D ** -0.5, 0.0625, ((0, 8), (1, 32)))
    down_weight = centred(seeds[4], (FF, D), FF ** -0.5, 0.03125, ((0, 32), (1, 8)))
    return dict(tokens=tokens, out_grad=out_grad, gate_weight=gate_weight, up_weight=up_weight, down_weight=down_weight)


def contract_first(left, right):
    return lax.dot_general(left, right, (((0,), (0,)), ((), ())), preferred_element_type=jnp.float32)


def contract_last(left, right):
    return lax.dot_general(left, right, (((1,), (1,)), ((), ())), preferred_element_type=jnp.float32)


def reference(tokens, out_grad, gate_weight, up_weight, down_weight):
    gate = jnp.dot(tokens, gate_weight, preferred_element_type=jnp.float32)
    up = jnp.dot(tokens, up_weight, preferred_element_type=jnp.float32)
    sig = jax.nn.sigmoid(gate)
    act = gate * sig
    hidden = (act * up).astype(jnp.bfloat16)
    hidden_grad = contract_last(out_grad, down_weight)
    gate_delta = (hidden_grad * up * sig * (1.0 + gate * (1.0 - sig))).astype(jnp.bfloat16)
    up_delta = (hidden_grad * act).astype(jnp.bfloat16)
    down_grad = contract_first(hidden, out_grad).astype(jnp.bfloat16)
    gate_grad = contract_first(tokens, gate_delta).astype(jnp.bfloat16)
    up_grad = contract_first(tokens, up_delta).astype(jnp.bfloat16)
    input_grad = (contract_last(gate_delta, gate_weight) + contract_last(up_delta, up_weight)).astype(jnp.bfloat16)
    return input_grad, gate_grad, up_grad, down_grad
```

```python
import jax
import jax.numpy as jnp
from jax import lax
from jax.sharding import PartitionSpec as P

BF16, F32 = jnp.bfloat16, jnp.float32
NX, NZ, NY = 4, 8, 4
Z_GROUPS = [[x * NZ + z for z in range(NZ)] for x in range(NX)]


def x_shift(k):
    return [(x * NZ + z, (x + k) % NX * NZ + z) for x in range(NX) for z in range(NZ)]


def y_shift(k):
    return [(y * 2 + c, (y + k) % NY * 2 + c) for y in range(NY) for c in range(2)]


CORE_SWAP = [(y * 2 + c, y * 2 + 1 - c) for y in range(NY) for c in range(2)]


def contract_first(left, right):
    return lax.dot_general(left, right, (((0,), (0,)), ((), ())), preferred_element_type=F32)


def contract_last(left, right):
    return lax.dot_general(left, right, (((1,), (1,)), ((), ())), preferred_element_type=F32)


def gather_z(block):
    copies = jnp.broadcast_to(block[None], (NZ,) + block.shape)
    got = lax.all_to_all(copies, "col", 0, 0, axis_index_groups=Z_GROUPS, tiled=True)
    return got.reshape(NZ * block.shape[0], block.shape[1])


def gather_x(plane):
    parts = [plane] + [lax.ppermute(plane, "col", x_shift(k)) for k in (1, 3, 2)]
    return jnp.concatenate(parts, axis=0)


def per_device(tokens, out_grad, gate_weight, up_weight, down_weight):
    width = gate_weight.shape[1]
    row = lax.axis_index("row")
    y, core = row // 2, row % 2
    token_panel = gather_x(gather_z(tokens))
    grad_panel = gather_x(gather_z(out_grad))
    count = token_panel.shape[0]
    half, quarter = count // 2, count // 8

    gate_part = jnp.dot(token_panel, gate_weight, preferred_element_type=F32)
    up_part = jnp.dot(token_panel, up_weight, preferred_element_type=F32)
    back_part = contract_last(grad_panel, down_weight)

    def sum_over_row(part):
        mine = lax.dynamic_slice_in_dim(part, core * half, half, 0)
        other = lax.dynamic_slice_in_dim(part, (1 - core) * half, half, 0)
        pair = mine + lax.ppermute(other, "row", CORE_SWAP)
        total = lax.dynamic_slice_in_dim(pair, y * quarter, quarter, 0)
        for k in (2, 1, 3):
            piece = lax.dynamic_slice_in_dim(pair, (y + k) % NY * quarter, quarter, 0)
            total = total + lax.ppermute(piece.astype(BF16), "row", y_shift(k)).astype(F32)
        return total

    gate, up, hidden_grad = (sum_over_row(part) for part in (gate_part, up_part, back_part))
    sig = jax.nn.sigmoid(gate)
    act = gate * sig
    hidden = (act * up).astype(BF16)
    gate_delta = (hidden_grad * up * sig * (1.0 + gate * (1.0 - sig))).astype(BF16)
    up_delta = (hidden_grad * act).astype(BF16)

    def gather_over_row(share):
        mine = jnp.zeros((half, share.shape[1]), BF16)
        mine = lax.dynamic_update_slice_in_dim(mine, share, y * quarter, 0)
        for k in (2, 1, 3):
            got = lax.ppermute(share, "row", y_shift(k))
            mine = lax.dynamic_update_slice_in_dim(mine, got, (y - k) % NY * quarter, 0)
        other = lax.ppermute(mine, "row", CORE_SWAP)
        return jnp.where(
            core == 0, jnp.concatenate([mine, other], 0), jnp.concatenate([other, mine], 0)
        )

    deltas = gather_over_row(jnp.concatenate([gate_delta, up_delta], axis=1))
    hidden = gather_over_row(hidden)
    gate_delta, up_delta = deltas[:, :width], deltas[:, width:]

    partial = contract_last(gate_delta, gate_weight) + contract_last(up_delta, up_weight)
    planes = partial.reshape(NX, count // NX, partial.shape[1])
    plane_sum = planes[0]
    for at, k in ((3, 2), (1, 3), (2, 1)):
        plane_sum = plane_sum + lax.ppermute(planes[at].astype(BF16), "col", x_shift(k)).astype(F32)
    pieces = plane_sum.reshape(NZ, count // (NX * NZ), partial.shape[1]).astype(BF16)
    pieces = lax.all_to_all(pieces, "col", 0, 0, axis_index_groups=Z_GROUPS, tiled=True)
    input_grad = jnp.sum(pieces.astype(F32), axis=0).astype(BF16)

    down_grad = contract_first(hidden, grad_panel).astype(BF16)
    gate_grad = contract_first(token_panel, gate_delta).astype(BF16)
    up_grad = contract_first(token_panel, up_delta).astype(BF16)
    return (input_grad, gate_grad, up_grad, down_grad)


def solution(mesh):
    return jax.shard_map(
        per_device,
        mesh=mesh,
        in_specs=(
            P("col", "row"),
            P("col", "row"),
            P("row", "col"),
            P("row", "col"),
            P("col", "row"),
        ),
        out_specs=(P("col", "row"), P("row", "col"), P("row", "col"), P("col", "row")),
        check_vma=False,
    )
```

```python
import jax
import jax.numpy as jnp
from jax import lax
from jax.sharding import PartitionSpec as P

BF16, F32 = jnp.bfloat16, jnp.float32
NX, NZ, NY = 4, 8, 4
FIRST, SECOND = (2, -2, 3, -3), (0, 1, -1, 4)


def x_shift(k):
    return [(x * NZ + z, (x + k) % NX * NZ + z) for x in range(NX) for z in range(NZ)]


def z_shift(k):
    return [(x * NZ + z, x * NZ + (z + k) % NZ) for x in range(NX) for z in range(NZ)]


def y_shift(k):
    return [(y * 2 + c, (y + k) % NY * 2 + c) for y in range(NY) for c in range(2)]


CORE_SWAP = [(y * 2 + c, y * 2 + 1 - c) for y in range(NY) for c in range(2)]


def contract_first(left, right):
    return lax.dot_general(left, right, (((0,), (0,)), ((), ())), preferred_element_type=F32)


def contract_last(left, right):
    return lax.dot_general(left, right, (((1,), (1,)), ((), ())), preferred_element_type=F32)


def after(value, *others):
    return lax.optimization_barrier((value,) + others)[0]


def per_device(tokens, out_grad, gate_weight, up_weight, down_weight):
    depth, width = gate_weight.shape
    row = lax.axis_index("row")
    y, core = row // 2, row % 2

    def cut(pair, k):
        quarter = pair.shape[0] // NY
        return lax.dynamic_slice_in_dim(pair, (y + k) % NY * quarter, quarter, 0)

    def by_core(mine, other):
        return jnp.where(core == 0, mine, other), jnp.where(core == 0, other, mine)

    def forward(rows):
        return [
            jnp.dot(rows[:, :depth], gate_weight, preferred_element_type=F32),
            jnp.dot(rows[:, :depth], up_weight, preferred_element_type=F32),
            contract_last(rows[:, depth:], down_weight),
        ]

    def swap_cores(part):
        return lax.ppermute(part, "row", CORE_SWAP)

    def panels_of(blocks):
        low, high = (jnp.concatenate(b, axis=0) for b in (blocks[:2], blocks[2:]))
        return by_core(low, high)

    def pair_of(mine, other):
        theirs = forward(other)
        return [m + swap_cores(t) for m, t in zip(forward(mine), theirs)]

    def sum_over_y(pair):
        pieces = [jnp.concatenate([cut(p, k).astype(BF16) for p in pair], axis=1) for k in (2, 1, 3)]
        got = [lax.ppermute(p, "row", y_shift(k)) for p, k in zip(pieces, (2, 1, 3))]
        return pieces, got

    def deltas_of(pair, got):
        gate, up, hidden_grad = (
            cut(p, 0) + sum(g[:, i * width : (i + 1) * width].astype(F32) for g in got)
            for i, p in enumerate(pair)
        )
        sig = jax.nn.sigmoid(gate)
        act = gate * sig
        hidden = (act * up).astype(BF16)
        gate_delta = (hidden_grad * up * sig * (1.0 + gate * (1.0 - sig))).astype(BF16)
        up_delta = (hidden_grad * act).astype(BF16)
        return jnp.concatenate([gate_delta, up_delta, hidden], axis=1)

    def send_share(share):
        return [lax.ppermute(share, "row", y_shift(k)) for k in (2, 1, 3)]

    def place(share, got):
        quarter = share.shape[0]
        mine = jnp.zeros((NY * quarter, share.shape[1]), BF16)
        mine = lax.dynamic_update_slice_in_dim(mine, share, y * quarter, 0)
        for k, g in zip((2, 1, 3), got):
            mine = lax.dynamic_update_slice_in_dim(mine, g, (y - k) % NY * quarter, 0)
        return mine

    def planes_of(mine, other):
        partials = [
            contract_last(d[:, :width], gate_weight)
            + contract_last(d[:, width : 2 * width], up_weight)
            for d in (mine, other)
        ]
        planes = jnp.concatenate(by_core(*partials), axis=0).reshape(4, NX, -1, depth)
        return planes[:, 0], [planes[:, at].astype(BF16) for at in (3, 1, 2)]

    def send_planes(planes):
        return [lax.ppermute(p, "col", x_shift(k)) for p, k in zip(planes, (2, 3, 1))]

    def send_rows(chunk, own, sent):
        total = own + sum(s.astype(F32) for s in sent)
        return [
            total[at] if k == 0 else lax.ppermute(total[at].astype(BF16), "col", z_shift(k))
            for at, k in enumerate(chunk)
        ]

    def weight_grads(panels, mine, other):
        panel = jnp.concatenate(panels, axis=0)
        delta = jnp.concatenate([mine, other], axis=0)
        return [
            contract_first(panel[:, :depth], delta[:, :width]),
            contract_first(panel[:, :depth], delta[:, width : 2 * width]),
            contract_first(delta[:, 2 * width :], panel[:, depth:]),
        ]

    both = jnp.concatenate([tokens, out_grad], axis=1)
    planes = [both] + [lax.ppermute(both, "col", x_shift(k)) for k in (1, 3, 2)]
    blocks = {0: jnp.concatenate(planes, axis=0)}
    for k in (1, 2, 3):
        blocks[-k] = lax.ppermute(blocks[1 - k], "col", z_shift(1))
        blocks[k] = lax.ppermute(blocks[k - 1], "col", z_shift(-1))
    left = lax.ppermute(blocks[-3][:, :depth], "col", z_shift(1))
    right = lax.ppermute(blocks[3][:, depth:], "col", z_shift(-1))
    blocks[4] = jnp.concatenate([left, right], axis=1)

    panels_1 = panels_of([blocks[k] for k in FIRST])
    pair_1 = pair_of(*panels_1)
    pieces_1, got_1 = sum_over_y(pair_1)
    panels_2 = panels_of(after([blocks[k] for k in SECOND], *pieces_1))
    pair_2 = pair_of(*panels_2)
    pieces_2, got_2 = sum_over_y(pair_2)
    share_1 = deltas_of(pair_1, after(got_1, *pieces_2))
    round_1 = send_share(share_1)
    share_2 = deltas_of(pair_2, after(got_2, share_1))
    round_2 = send_share(share_2)

    mine_1 = place(share_1, after(round_1, share_2))
    other_1 = swap_cores(mine_1)
    own_1, planes_1 = planes_of(mine_1, other_1)
    sent_1 = send_planes(planes_1)
    mine_2 = place(share_2, after(round_2, *planes_1))
    other_2 = swap_cores(mine_2)
    own_2, planes_2 = planes_of(mine_2, other_2)
    sent_2 = send_planes(planes_2)
    grads_1 = weight_grads(after(panels_1, *planes_1), mine_1, other_1)
    rows_1 = send_rows(FIRST, own_1, after(sent_1, *planes_2))
    grads_2 = weight_grads(after(panels_2, *planes_2), mine_2, other_2)
    rows_2 = send_rows(SECOND, own_2, sent_2)
    input_grad = sum(r.astype(F32) for r in rows_1 + rows_2).astype(BF16)
    return (input_grad,) + tuple((a + b).astype(BF16) for a, b in zip(grads_1, grads_2))


def solution(mesh):
    return jax.shard_map(
        per_device,
        mesh=mesh,
        in_specs=(
            P("col", "row"),
            P("col", "row"),
            P("row", "col"),
            P("row", "col"),
            P("col", "row"),
        ),
        out_specs=(P("col", "row"), P("row", "col"), P("row", "col"), P("col", "row")),
        check_vma=False,
    )
```

```python
import jax
import jax.numpy as jnp
from jax import lax
from jax.sharding import PartitionSpec as P

BF16, F32 = jnp.bfloat16, jnp.float32
NX, NZ, NY = 4, 8, 4
FIRST, SECOND = (2, 3, -2, -3), (0, 1, -1, 4)


def x_shift(k):
    return [(x * NZ + z, (x + k) % NX * NZ + z) for x in range(NX) for z in range(NZ)]


def z_shift(k):
    return [(x * NZ + z, x * NZ + (z + k) % NZ) for x in range(NX) for z in range(NZ)]


def y_shift(k):
    return [(y * 2 + c, (y + k) % NY * 2 + c) for y in range(NY) for c in range(2)]


CORE_SWAP = [(y * 2 + c, y * 2 + 1 - c) for y in range(NY) for c in range(2)]


def contract_first(left, right):
    return lax.dot_general(left, right, (((0,), (0,)), ((), ())), preferred_element_type=F32)


def contract_last(left, right):
    return lax.dot_general(left, right, (((1,), (1,)), ((), ())), preferred_element_type=F32)


def after(value, *others):
    return lax.optimization_barrier((value,) + others)[0]


def per_device(tokens, out_grad, gate_weight, up_weight, down_weight):
    depth, width = gate_weight.shape
    row = lax.axis_index("row")
    y, core = row // 2, row % 2

    def cut(pair, k):
        quarter = pair.shape[0] // NY
        return lax.dynamic_slice_in_dim(pair, (y + k) % NY * quarter, quarter, 0)

    def by_core(mine, other):
        return jnp.where(core == 0, mine, other), jnp.where(core == 0, other, mine)

    def forward(rows):
        return [
            jnp.dot(rows[:, :depth], gate_weight, preferred_element_type=F32),
            jnp.dot(rows[:, :depth], up_weight, preferred_element_type=F32),
            contract_last(rows[:, depth:], down_weight),
        ]

    def swap_cores(part):
        return lax.ppermute(part, "row", CORE_SWAP)

    def panels_of(blocks):
        low, high = (jnp.concatenate(b, axis=0) for b in (blocks[:2], blocks[2:]))
        return by_core(low, high)

    def pair_of(mine, other):
        theirs = forward(other)
        return [m + swap_cores(t) for m, t in zip(forward(mine), theirs)]

    def sum_over_y(pair):
        pieces = [jnp.concatenate([cut(p, k).astype(BF16) for p in pair], axis=1) for k in (2, 1, 3)]
        got = [lax.ppermute(p, "row", y_shift(k)) for p, k in zip(pieces, (2, 1, 3))]
        return pieces, got

    def deltas_of(pair, got):
        gate, up, hidden_grad = (
            cut(p, 0) + sum(g[:, i * width : (i + 1) * width].astype(F32) for g in got)
            for i, p in enumerate(pair)
        )
        sig = jax.nn.sigmoid(gate)
        act = gate * sig
        hidden = (act * up).astype(BF16)
        gate_delta = (hidden_grad * up * sig * (1.0 + gate * (1.0 - sig))).astype(BF16)
        up_delta = (hidden_grad * act).astype(BF16)
        return jnp.concatenate([gate_delta, up_delta, hidden], axis=1)

    def send_share(share):
        return [lax.ppermute(share, "row", y_shift(k)) for k in (2, 1, 3)]

    def place(share, got):
        quarter = share.shape[0]
        mine = jnp.zeros((NY * quarter, share.shape[1]), BF16)
        mine = lax.dynamic_update_slice_in_dim(mine, share, y * quarter, 0)
        for k, g in zip((2, 1, 3), got):
            mine = lax.dynamic_update_slice_in_dim(mine, g, (y - k) % NY * quarter, 0)
        return mine

    def planes_of(mine, other):
        partials = [
            contract_last(d[:, :width], gate_weight)
            + contract_last(d[:, width : 2 * width], up_weight)
            for d in (mine, other)
        ]
        planes = jnp.concatenate(by_core(*partials), axis=0).reshape(4, NX, -1, depth)
        return planes[:, 0], [planes[:, at].astype(BF16) for at in (3, 1, 2)]

    def send_planes(planes):
        return [lax.ppermute(p, "col", x_shift(k)) for p, k in zip(planes, (2, 3, 1))]

    def sum_planes(own, sent):
        return own + sum(s.astype(F32) for s in sent)

    def weight_grads(panels, mine, other):
        panel = jnp.concatenate(panels, axis=0)
        delta = jnp.concatenate([mine, other], axis=0)
        return [
            contract_first(panel[:, :depth], delta[:, :width]),
            contract_first(panel[:, :depth], delta[:, width : 2 * width]),
            contract_first(delta[:, 2 * width :], panel[:, depth:]),
        ]

    both = jnp.concatenate([tokens, out_grad], axis=1)
    planes = [both] + [lax.ppermute(both, "col", x_shift(k)) for k in (1, 3, 2)]
    blocks = {0: jnp.concatenate(planes, axis=0)}
    for k in (1, 2, 3):
        blocks[-k] = lax.ppermute(blocks[1 - k], "col", z_shift(1))
        blocks[k] = lax.ppermute(blocks[k - 1], "col", z_shift(-1))
    left = lax.ppermute(blocks[-3][:, :depth], "col", z_shift(1))
    right = lax.ppermute(blocks[3][:, depth:], "col", z_shift(-1))
    blocks[4] = jnp.concatenate([left, right], axis=1)

    panels_1 = panels_of([blocks[k] for k in FIRST])
    pair_1 = pair_of(*panels_1)
    pieces_1, got_1 = sum_over_y(pair_1)
    panels_2 = panels_of(after([blocks[k] for k in SECOND], *pieces_1))
    pair_2 = pair_of(*panels_2)
    pieces_2, got_2 = sum_over_y(pair_2)
    share_1 = deltas_of(pair_1, after(got_1, *pieces_2))
    round_1 = send_share(share_1)
    share_2 = deltas_of(pair_2, after(got_2, share_1))
    round_2 = send_share(share_2)

    mine_1 = place(share_1, after(round_1, share_2))
    other_1 = swap_cores(mine_1)
    own_1, planes_1 = planes_of(mine_1, other_1)
    sent_1 = send_planes(planes_1)
    mine_2 = place(share_2, after(round_2, *planes_1))
    other_2 = swap_cores(mine_2)
    own_2, planes_2 = planes_of(mine_2, other_2)
    sent_2 = send_planes(planes_2)
    grads_1 = weight_grads(after(panels_1, *planes_1), mine_1, other_1)
    total_1 = sum_planes(own_1, after(sent_1, *planes_2)).astype(BF16)
    up = lax.ppermute(total_1[:2], "col", z_shift(2)).astype(F32)
    down = lax.ppermute(total_1[2:], "col", z_shift(-2)).astype(F32)
    grads_2 = weight_grads(after(panels_2, *planes_2), mine_2, other_2)
    total_2 = sum_planes(own_2, sent_2)
    rows = [
        lax.ppermute(total_2[3], "col", z_shift(4)),
        lax.ppermute(total_2[1] + up[1], "col", z_shift(1)),
        lax.ppermute(total_2[2] + down[1], "col", z_shift(-1)),
    ]
    input_grad = (total_2[0] + up[0] + down[0] + sum(rows)).astype(BF16)
    return (input_grad,) + tuple((a + b).astype(BF16) for a, b in zip(grads_1, grads_2))


def solution(mesh):
    return jax.shard_map(
        per_device,
        mesh=mesh,
        in_specs=(
            P("col", "row"),
            P("col", "row"),
            P("row", "col"),
            P("row", "col"),
            P("col", "row"),
        ),
        out_specs=(P("col", "row"), P("row", "col"), P("row", "col"), P("col", "row")),
        check_vma=False,
    )
```

```python
import jax
import jax.numpy as jnp
from jax import lax
from jax.sharding import PartitionSpec as P

BF16, F32 = jnp.bfloat16, jnp.float32
NX, NZ, NY = 4, 8, 4
FIRST, SECOND = (2, 3, -2, -3), (0, 1, -1, 4)


def x_shift(k):
    return [(x * NZ + z, (x + k) % NX * NZ + z) for x in range(NX) for z in range(NZ)]


def z_shift(k):
    return [(x * NZ + z, x * NZ + (z + k) % NZ) for x in range(NX) for z in range(NZ)]


def y_shift(k):
    return [(y * 2 + c, (y + k) % NY * 2 + c) for y in range(NY) for c in range(2)]


CORE_SWAP = [(y * 2 + c, y * 2 + 1 - c) for y in range(NY) for c in range(2)]


def contract_first(left, right):
    return lax.dot_general(left, right, (((0,), (0,)), ((), ())), preferred_element_type=F32)


def contract_last(left, right):
    return lax.dot_general(left, right, (((1,), (1,)), ((), ())), preferred_element_type=F32)


def after(value, *others):
    return lax.optimization_barrier((value,) + others)[0]


def per_device(tokens, out_grad, gate_weight, up_weight, down_weight):
    depth, width = gate_weight.shape
    row = lax.axis_index("row")
    y, core = row // 2, row % 2

    def cut(pair, k):
        quarter = pair.shape[0] // NY
        return lax.dynamic_slice_in_dim(pair, (y + k) % NY * quarter, quarter, 0)

    def by_core(mine, other):
        return jnp.where(core == 0, mine, other), jnp.where(core == 0, other, mine)

    def forward(rows):
        return [
            jnp.dot(rows[:, :depth], gate_weight, preferred_element_type=F32),
            jnp.dot(rows[:, :depth], up_weight, preferred_element_type=F32),
            contract_last(rows[:, depth:], down_weight),
        ]

    def swap_cores(part):
        return lax.ppermute(part, "row", CORE_SWAP)

    def panels_of(blocks):
        low, high = (jnp.concatenate(b, axis=0) for b in (blocks[:2], blocks[2:]))
        return by_core(low, high)

    def pair_of(mine, other):
        theirs = forward(other)
        return [m + swap_cores(t) for m, t in zip(forward(mine), theirs)]

    def sum_over_y(pair):
        pieces = [jnp.concatenate([cut(p, k).astype(BF16) for p in pair], axis=1) for k in (1, 3, 2)]
        got = [lax.ppermute(p, "row", y_shift(k)) for p, k in zip(pieces, (1, 3, 2))]
        return pieces, got

    def deltas_of(pair, got):
        gate, up, hidden_grad = (
            cut(p, 0) + sum(g[:, i * width : (i + 1) * width].astype(F32) for g in got)
            for i, p in enumerate(pair)
        )
        sig = jax.nn.sigmoid(gate)
        act = gate * sig
        hidden = (act * up).astype(BF16)
        gate_delta = (hidden_grad * up * sig * (1.0 + gate * (1.0 - sig))).astype(BF16)
        up_delta = (hidden_grad * act).astype(BF16)
        return jnp.concatenate([gate_delta, up_delta, hidden], axis=1)

    def send_share(share):
        return [lax.ppermute(share, "row", y_shift(k)) for k in (1, 3, 2)]

    def place(share, got):
        quarter = share.shape[0]
        mine = jnp.zeros((NY * quarter, share.shape[1]), BF16)
        mine = lax.dynamic_update_slice_in_dim(mine, share, y * quarter, 0)
        for k, g in zip((1, 3, 2), got):
            mine = lax.dynamic_update_slice_in_dim(mine, g, (y - k) % NY * quarter, 0)
        return mine

    def planes_of(mine, other):
        partials = [
            contract_last(d[:, :width], gate_weight)
            + contract_last(d[:, width : 2 * width], up_weight)
            for d in (mine, other)
        ]
        planes = jnp.concatenate(by_core(*partials), axis=0).reshape(4, NX, -1, depth)
        return planes[:, 0], [planes[:, at].astype(BF16) for at in (3, 1, 2)]

    def send_planes(planes):
        return [lax.ppermute(p, "col", x_shift(k)) for p, k in zip(planes, (2, 3, 1))]

    def sum_planes(own, sent):
        return own + sum(s.astype(F32) for s in sent)

    def weight_grads(panels, mine, other):
        panel = jnp.concatenate(panels, axis=0)
        delta = jnp.concatenate([mine, other], axis=0)
        return [
            contract_first(panel[:, :depth], delta[:, :width]),
            contract_first(panel[:, :depth], delta[:, width : 2 * width]),
            contract_first(delta[:, 2 * width :], panel[:, depth:]),
        ]

    low = jnp.array(-jnp.inf, BF16)
    both = jnp.maximum(
        lax.pad(tokens, low, ((0, 0, 0), (0, depth, 0))),
        lax.pad(out_grad, low, ((0, 0, 0), (depth, 0, 0))),
    )
    planes = [both] + [lax.ppermute(both, "col", x_shift(k)) for k in (1, 3, 2)]
    blocks = {0: jnp.concatenate(planes, axis=0)}
    for k in (1, 2, 3):
        blocks[-k] = lax.ppermute(blocks[1 - k], "col", z_shift(1))
        blocks[k] = lax.ppermute(blocks[k - 1], "col", z_shift(-1))
    left = lax.ppermute(blocks[-3][:, :depth], "col", z_shift(1))
    right = lax.ppermute(blocks[3][:, depth:], "col", z_shift(-1))
    blocks[4] = jnp.concatenate([left, right], axis=1)

    panels_1 = panels_of([blocks[k] for k in FIRST])
    pair_1 = pair_of(*panels_1)
    pieces_1, got_1 = sum_over_y(pair_1)
    panels_2 = panels_of(after([blocks[k] for k in SECOND], *pieces_1))
    pair_2 = pair_of(*panels_2)
    pieces_2, got_2 = sum_over_y(pair_2)
    share_1 = deltas_of(pair_1, after(got_1, *pieces_2))
    round_1 = send_share(share_1)
    share_2 = deltas_of(pair_2, after(got_2, share_1))
    round_2 = send_share(share_2)

    mine_1 = place(share_1, after(round_1, share_2))
    other_1 = swap_cores(mine_1)
    own_1, planes_1 = planes_of(mine_1, other_1)
    sent_1 = send_planes(planes_1)
    mine_2 = place(share_2, after(round_2, *planes_1))
    other_2 = swap_cores(mine_2)
    own_2, planes_2 = planes_of(mine_2, other_2)
    sent_2 = send_planes(planes_2)
    grads_1 = weight_grads(after(panels_1, *planes_1), mine_1, other_1)
    total_1 = sum_planes(own_1, after(sent_1, *planes_2)).astype(BF16)
    up = lax.ppermute(total_1[:2], "col", z_shift(2)).astype(F32)
    down = lax.ppermute(total_1[2:], "col", z_shift(-2)).astype(F32)
    grads_2 = weight_grads(after(panels_2, *planes_2), mine_2, other_2)
    total_2 = sum_planes(own_2, sent_2)
    rows = [
        lax.ppermute(total_2[3], "col", z_shift(4)),
        lax.ppermute(total_2[1] + up[1], "col", z_shift(1)),
        lax.ppermute(total_2[2] + down[1], "col", z_shift(-1)),
    ]
    input_grad = (total_2[0] + up[0] + down[0] + sum(rows)).astype(BF16)
    return (input_grad,) + tuple((a + b).astype(BF16) for a, b in zip(grads_1, grads_2))


def solution(mesh):
    return jax.shard_map(
        per_device,
        mesh=mesh,
        in_specs=(
            P("col", "row"),
            P("col", "row"),
            P("row", "col"),
            P("row", "col"),
            P("col", "row"),
        ),
        out_specs=(P("col", "row"), P("row", "col"), P("row", "col"), P("col", "row")),
        check_vma=False,
    )
```
